256 devices in a mesh: rep: 32 (over z, x_hi, core), exp: 8 (over x_lo, y).
Axes of the slice: x: 4 (x_hi: 2, x_lo: 2; x = x_hi * 2 + x_lo), y: 4, z: 8, core: 2. Of those that a mesh axis runs over, the one named last changes fastest.
Arguments:
- tokens: bfloat16 [24576, 7168], P('rep'), may hold values from -6 to 6
- gates: float32 [24576, 8], P('rep'), may hold values from 0.1 to 1
- assign: int32 [24576, 8], P('rep'), may hold values from 0 to 7, each once within a row
- master: float32 [8, 224, 128, 256], P('exp', 'rep')
- owner: int32 [8, 224], P('exp'), may hold values from 0 to 31, as said below
Outputs:
- combined: bfloat16 [24576, 1024], P(('rep', 'exp'))
The draws below stay inside these ranges and needn't reach their ends.
Inputs may be any that keep to these rules, and one draw needn't show every extreme that they name: `owner`: in each row, every index of rep owns exactly 7 buckets.
All inputs are finite; a program needn't handle non-finite values.
Results may differ from the reference program's by a relative error of at most 0.001.
Values may be sent and summed in bfloat16 or wider, within the bound.
A program may use at most 192 MiB of HBM per device.

```python
import math
import jax
import jax.numpy as jnp
from jax import lax

D = 7168
FW = 1024
BLK = 128
EXPERTS = 8
BUCKETS = 224
TOKENS = 24576
N_REP = 32


def draw_master(key, part):
    key = jax.random.fold_in(key, 11)
    base_key, row_key, col_key = jax.random.split(key, 3)
    full_shape = (EXPERTS, BUCKETS, BLK, 2 * BLK)
    base = jax.random.normal(base_key, full_shape, jnp.float32)
    row_factor = jnp.exp(jax.random.uniform(row_key, (EXPERTS, BUCKETS, BLK, 1), jnp.float32, -1.15, 1.15))
    col_factor = jnp.exp(jax.random.uniform(col_key, (EXPERTS, BUCKETS, 1, 2 * BLK), jnp.float32, -1.15, 1.15))
    return base * row_factor * col_factor * D ** (-0.5)


def owner_table_row(row_key):
    return jax.random.permutation(row_key, BUCKETS) // (BUCKETS // N_REP)


def draw_owner(key, part):
    key = jax.random.fold_in(key, 7)
    row_keys = jax.random.split(key, EXPERTS)
    return jax.vmap(owner_table_row)(row_keys).astype(jnp.int32)


def steps_of(rng, extent, cuts, low, top_value):
    level = 1.0
    for dim, parts in cuts:
        heights = jax.random.uniform(jax.random.fold_in(jax.random.fold_in(rng, 6), dim), (parts,), jnp.float32, low / len(cuts), top_value / len(cuts))
        level = level * jnp.repeat(jnp.exp(heights), extent[dim] // parts).reshape((-1,) + (1,) * (len(extent) - 1 - dim))
    return level


def scatter_about(rng, shape, spread, most, cuts=(), kind=jnp.bfloat16):
    level = steps_of(rng, shape, cuts, -0.22, 0.18) if cuts else 1.0
    values = jax.random.normal(rng, shape, jnp.float32) * spread * level
    return jnp.minimum(jnp.maximum(values, -most), most).astype(kind)


def setup_inputs(seed: int = 0) -> dict:
    splits = jax.random.split(jax.random.key(seed), 6)
    return {
        "tokens": scatter_about(splits[0], (TOKENS, D), 1.0, 6.0, ((0, 32),)),
        "gates": jnp.clip(jnp.exp(math.log(1.0) - 2.3025851 * jax.random.uniform(splits[1], (TOKENS, EXPERTS), jnp.float32) ** steps_of(splits[1], (TOKENS, EXPERTS), ((0, 32),), -0.2, 0.2)), 0.1, 1.0),
        "assign": jax.vmap(lambda own: jax.random.permutation(own, EXPERTS))(jax.random.split(splits[2], TOKENS)).reshape((TOKENS, EXPERTS)).astype(jnp.int32),
        "master": draw_master(jax.random.fold_in(splits[5], 71), 0),
        "owner": draw_owner(jax.random.fold_in(splits[5], 71), 0),
    }


QUANT_LIMIT = 448.0
GRID_STEP = 16.0


def nearest_even(scaled):
    shifted = scaled / GRID_STEP + 0.5
    level = jnp.floor(shifted)
    halfway = shifted == level
    odd_level = (level - 2.0 * jnp.floor(level * 0.5)) == 1.0
    level = jnp.where(jnp.logical_and(halfway, odd_level), level - 1.0, level)
    return level * GRID_STEP


def serve_tiles(master_slots):
    slot_count = master_slots.shape[0]
    blocks_view = master_slots.reshape(slot_count, BLK, 2, BLK)
    block_peak = jnp.max(jnp.abs(blocks_view), axis=(1, 3))
    block_scale = jnp.full_like(block_peak, 2.0 ** -30)
    reciprocal = jnp.full_like(block_peak, 2.0 ** 30)
    for exponent in range(-30, 1):
        exceeds = block_peak > QUANT_LIMIT * (2.0 ** exponent)
        block_scale = jnp.where(exceeds, 2.0 ** (exponent + 1), block_scale)
        reciprocal = jnp.where(exceeds, 2.0 ** (-exponent - 1), reciprocal)
    scaled = blocks_view * reciprocal[:, None, :, None]
    quantized = nearest_even(scaled)
    served_tile = (quantized * block_scale[:, None, :, None]).astype(jnp.bfloat16)
    return jnp.transpose(served_tile, (0, 2, 3, 1)).reshape(slot_count, 2 * BLK, BLK)


def build_weight(master_slots, owner_line):
    slot_bucket = jnp.argsort(owner_line, stable=True).astype(jnp.int32)
    served_tiles = serve_tiles(master_slots)
    placed = jnp.zeros_like(served_tiles).at[slot_bucket].set(served_tiles)
    groups = FW // (2 * BLK)
    placed = placed.reshape(D // BLK, groups, 2 * BLK, BLK)
    return jnp.transpose(placed, (0, 3, 1, 2)).reshape(D, FW)


def reference(tokens, gates, assign, master, owner):
    def one_shard(running, inputs):
        master_slots, owner_line, shard_index = inputs
        weight = build_weight(master_slots, owner_line)
        gate_pick = jnp.sum(jnp.where(assign == shard_index, gates, jnp.zeros_like(gates)), axis=1)
        projection = jnp.dot(tokens, weight, preferred_element_type=jnp.float32)
        return running + gate_pick[:, None] * projection, None

    zero_sum = jnp.zeros((TOKENS, FW), jnp.float32)
    shard_ids = jnp.arange(EXPERTS, dtype=jnp.int32)
    combined, unused = lax.scan(one_shard, zero_sum, (master, owner, shard_ids))
    return combined.astype(jnp.bfloat16)
```

```python
import functools

import jax
import jax.numpy as jnp
from jax import lax
from jax.experimental import pallas as pl
from jax.experimental.pallas import tpu as pltpu
from jax.sharding import PartitionSpec as P

D = 7168
FW = 1024
BLK = 128
SLOTS = 7
TOK = 768
ROWS = 96
PARTS = 8
PIECE = 2 * BLK // PARTS
OFFSETS = (0, 1, 3, 2)
PANELS = 8
CHUNKS = D // (BLK * PANELS)

QUANT_LIMIT = 448.0
GRID_STEP = 16.0
MESH = pl.DeviceIdType.MESH
NT = (((1,), (1,)), ((), ()))


def nearest_even(scaled):
    shifted = scaled * (1.0 / GRID_STEP) + 0.5
    level = jnp.floor(shifted)
    halfway = shifted == level
    odd_level = level - 2.0 * jnp.floor(level * 0.5) == 1.0
    level = jnp.where(jnp.logical_and(halfway, odd_level), level - 1.0, level)
    return level * GRID_STEP


def quantize(master_ref, peak_ref, recip_ref, pieces_ref):
    peak_ref[...] = jnp.zeros_like(peak_ref)
    for j in range(SLOTS):
        top = jnp.max(jnp.abs(master_ref[0, j]), axis=0, keepdims=True)
        for half in range(2):
            peak_ref[2 * j + half : 2 * j + half + 1, :] = top[:, half * BLK : (half + 1) * BLK]
    peak = jnp.broadcast_to(jnp.max(peak_ref[...], axis=1, keepdims=True), peak_ref.shape)
    scale = jnp.full_like(peak, 2.0**-30)
    recip = jnp.full_like(peak, 2.0**30)
    for exponent in range(-30, 1):
        exceeds = peak > QUANT_LIMIT * 2.0**exponent
        scale = jnp.where(exceeds, 2.0 ** (exponent + 1), scale)
        recip = jnp.where(exceeds, 2.0 ** (-exponent - 1), recip)
    peak_ref[...] = scale
    recip_ref[...] = recip
    for j in range(SLOTS):
        for half in range(2):
            r = 2 * j + half
            scaled = master_ref[0, j, :, half * BLK : (half + 1) * BLK] * recip_ref[r : r + 1, :]
            served = nearest_even(scaled) * peak_ref[r : r + 1, :]
            turned = served.T.astype(jnp.bfloat16)
            for q in range(PARTS // 2):
                pieces_ref[half * (PARTS // 2) + q, j] = turned[q * PIECE : (q + 1) * PIECE, :]


def slot_positions(owner):
    buckets = owner.shape[1]
    rows = lax.broadcasted_iota(jnp.int32, (buckets, buckets), 0)
    cols = lax.broadcasted_iota(jnp.int32, (buckets, buckets), 1)
    across = jnp.broadcast_to(owner, (buckets, buckets))
    down = jnp.sum(jnp.where(rows == cols, across, 0), axis=1, keepdims=True)
    earlier = jnp.logical_and(across == down, rows < cols)
    rank = jnp.sum(jnp.where(earlier, 1, 0), axis=0, keepdims=True)
    place = (owner & ~3) + ((owner & 1) << 1) + ((owner >> 1) & 1)
    return jnp.clip(place * SLOTS + rank, 0, buckets - 1)


def kernel(
    tokens_hbm, gates_ref, assign_ref, master_ref, owner_ref, out_ref,
    tok, w0, w1, w2, w3, pieces, peak, recip, line, lines, index, gate, partial, total, send_out, got_out,
    tok_sem, idx_sem,
    s_line, r_line, s_ex, r_ex, s_z, r_z, s_d, r_d, s_s, r_s, s_c, r_c, s_out, r_out,
):
    weights = (w0, w1, w2, w3)
    rep = lax.axis_index("rep")
    ex = lax.axis_index("exp")
    z, xh, c = rep // 4, (rep // 2) % 2, rep % 2
    xl, y = ex // 4, ex % 4
    half = (xl + xh) % 2
    part = half * 4 + y

    def dev(z_, xh_, c_, xl_, y_):
        return (z_ * 4 + xh_ * 2 + c_, xl_ * 4 + y_)

    up = dev((z + 1) % 8, xh, c, xl, y)
    down = dev((z + 7) % 8, xh, c, xl, y)
    side = dev(z, 1 - xh, c, 1 - xl, y)
    twin = dev(z, xh, 1 - c, xl, y)
    peers = [dev(z, xh, c, (xl + (n // 4)) % 2, (y + n) % 4) for n in range(1, 8)]

    barrier = pltpu.get_barrier_semaphore()
    for device in [up, down, side, twin] + peers:
        pl.semaphore_signal(barrier, inc=1, device_id=device, device_id_type=MESH)

    tok_copy = pltpu.make_async_copy(tokens_hbm, tok, tok_sem)
    tok_copy.start()
    quantize(master_ref, peak, recip, pieces)
    pl.semaphore_wait(barrier, 11)

    def send(src, dst, s_sem, r_sem, device):
        pltpu.make_async_remote_copy(
            src_ref=src, dst_ref=dst, send_sem=s_sem, recv_sem=r_sem, device_id=device, device_id_type=MESH
        ).start()

    def wait_slots(sem, n):
        ref = w0.at[0, pl.ds(0, n)]
        pltpu.make_async_copy(ref, ref, sem).wait()

    def base(z_):
        return ((z_ % 8) * 2 + c) * 14

    own = base(z) + 7 * xh
    at_s = 10 * xh
    at_d = 4 + 3 * xh
    at_d_side = 7 - 3 * xh
    at_ten = 4 * xh

    def sub(u):
        return (u + xh) % 2

    weights[0][xh, pl.ds(own, 7)] = pieces[part]
    for k in range(4):
        y_to = (y + 4 - OFFSETS[k]) % 4
        for j in range(2):
            if k == 0 and j == 1:
                continue
            xl_to = 1 - xl if k == 0 else (xl + j) % 2
            half_to = (xl_to + xh) % 2
            sub_to = (half_to + xl) % 2
            send(pieces.at[half_to * 4 + y_to], weights[k].at[sub_to, pl.ds(own, 7)], s_ex, r_ex.at[k],
                 dev(z, xh, c, xl_to, y_to))
        if k == 0:
            w = weights[0]
            send(w.at[xh, pl.ds(own, 7)], w.at[xh, pl.ds(own, 7)], s_z.at[0], r_z.at[0, 0], up)
            send(w.at[xh, pl.ds(own, 7)], w.at[xh, pl.ds(own, 7)], s_z.at[0], r_z.at[0, 0], down)
            ref = w.at[xh, pl.ds(base(z) + at_d, 3)]
            send(ref, ref, s_d.at[0], r_d.at[0], side)
            ref = w.at[xh, pl.ds(base(z) + at_s, 4)]
            send(ref, ref, s_s.at[0], r_s.at[0, 0], side)

    line[...] = jnp.zeros_like(line)
    line[:, 0:224] = slot_positions(owner_ref[...])
    lines[xh] = line[...]
    for k in range(4):
        y_to = (y + 4 - OFFSETS[k]) % 4
        for j in range(2):
            if k == 0 and j == 1:
                continue
            xl_to = 1 - xl if k == 0 else (xl + j) % 2
            sub_to = (xl_to + xh + xl) % 2
            send(line, lines.at[2 * k + sub_to], s_line, r_line, dev(z, xh, c, xl_to, y_to))

    def ring(u, lo, n, device, h):
        w = weights[u // 2]
        ref = w.at[sub(u), pl.ds(lo, n)]
        send(ref, ref, s_z.at[u], r_z.at[u, h], device)

    def over_side(u, z_, d):
        w = weights[u // 2]
        ref = w.at[sub(u), pl.ds(base(z_) + at_s, 4)]
        send(ref, ref, s_s.at[u], r_s.at[u, d], side)

    def exchange_d(k):
        if k == 0:
            return
        wait_slots(r_ex.at[k], 14)
        ref = weights[k].at[:, pl.ds(base(z) + at_d, 3)]
        send(ref, ref, s_d.at[2 * k], r_d.at[2 * k], side)

    def hop(u, h):
        if h == 1:
            if u >= 2:
                if u % 2 == 0:
                    wait_slots(r_d.at[u], 6)
                ring(u, base(z) + at_ten, 10, up, 0)
                ring(u, base(z) + at_ten, 10, down, 0)
                over_side(u, z, 0)
            elif u == 1:
                wait_slots(r_ex.at[0], 7)
                ring(1, own, 7, up, 0)
                ring(1, own, 7, down, 0)
                ref = weights[0].at[1 - xh, pl.ds(base(z) + at_d, 3)]
                send(ref, ref, s_d.at[1], r_d.at[1], side)
                over_side(1, z, 0)
                wait_slots(r_d.at[0], 3)
                ring(1, base(z) + at_d_side, 3, up, 0)
                ring(1, base(z) + at_d_side, 3, down, 0)
                wait_slots(r_d.at[1], 3)
                ring(0, base(z) + at_d_side, 3, up, 0)
                ring(0, base(z) + at_d_side, 3, down, 0)
            return
        d = h - 1
        if d <= 3:
            wait_slots(r_z.at[u, d - 1], 20)
            if h <= 3:
                ring(u, base(z + 8 - d) + at_ten, 10, up, d)
                ring(u, base(z + d) + at_ten, 10, down, d)
            else:
                ring(u, base(z + 8 - d) + 9 * xh, 5, up, d)
                ring(u, base(z + d) + 5 - xh, 5, down, d)
            over_side(u, z + 8 - d, d)
            over_side(u, z + d, d)
        else:
            wait_slots(r_z.at[u, 3], 10)
            over_side(u, z + 4, 4)

    def to_twin(k, d):
        n = 4 if d in (0, 4) else 8
        wait_slots(r_s.at[2 * k, d], n)
        wait_slots(r_s.at[2 * k + 1, d], n)
        for z_ in [z + d] if d in (0, 4) else [z + d, z + 8 - d]:
            ref = weights[k].at[:, pl.ds(base(z_), 14)]
            send(ref, ref, s_c.at[k], r_c.at[k], twin)

    def gates_of(u):
        e = ((half + u) % 2) * 4 + (y + OFFSETS[u // 2]) % 4
        pick = jnp.where(assign_ref[...] == e, gates_ref[...], 0.0)
        gate[u] = jnp.broadcast_to(jnp.sum(pick, axis=1, keepdims=True), (TOK, BLK))

    def chunks(k, lo, hi):
        w = weights[k]

        def body(ch, carry):
            tiles = []
            for i in range(PANELS):
                bucket = (ch * PANELS + i) * 4
                tiles.append(jnp.concatenate(
                    [w[s, index[2 * k + s, 0, bucket + g]] for s in range(2) for g in range(4)], axis=0))
            cols = pl.ds(pl.multiple_of(ch * (PANELS * BLK), PANELS * BLK), PANELS * BLK)
            partial[...] += lax.dot_general(
                tok[:, cols], jnp.concatenate(tiles, axis=1), NT, preferred_element_type=jnp.float32)
            return carry

        if lo == 0:
            wait_slots(r_c.at[k], 224)
            partial[...] = jnp.zeros_like(partial)
        lax.fori_loop(lo, hi, body, 0)
        if hi == CHUNKS:
            term = gate[2 * k] * partial[:, 0:BLK] + gate[2 * k + 1] * partial[:, BLK : 2 * BLK]
            total[...] = term if k == 0 else total[...] + term

    hop(1, 1)
    hop(0, 2)
    exchange_d(1)
    hop(1, 2)
    to_twin(0, 0)
    hop(0, 3)
    for u in range(4):
        gates_of(u)
    hop(2, 1)
    hop(0, 4)
    for u in range(4, 8):
        gates_of(u)
    wait_line = lines.at[pl.ds(0, 7)]
    pltpu.make_async_copy(wait_line, wait_line, r_line).wait()
    idx_copy = pltpu.make_async_copy(lines, index, idx_sem)
    idx_copy.start()
    idx_copy.wait()
    tok_copy.wait()

    work = [(k, lo, lo + 1) for k in range(4) for lo in range(CHUNKS)]
    ready = {0: 6, 1: 8, 2: 10, 3: 12}
    done = [0]

    def some_work(r, n):
        while n > 0 and done[0] < len(work) and r >= ready[work[done[0]][0]]:
            k, lo, hi = work[done[0]]
            m = 1
            while m < n and lo + m < CHUNKS:
                m += 1
            chunks(k, lo, lo + m)
            done[0] += m
            n -= m

    for r in range(3, 13):
        if r % 2 == 1 and (r + 1) // 2 < 4:
            exchange_d((r + 1) // 2)
        for h in range(6, 0, -1):
            u = r - (h - 1)
            if not 0 <= u < 8:
                continue
            if (r, h) == (3, 4):
                continue
            if h <= 5:
                hop(u, h)
            if u % 2 == 1 and h >= 2:
                to_twin(u // 2, h - 2)
            if h in (5, 3, 1):
                some_work(r, 2)
    some_work(99, 100)

    send_out[...] = total[...].astype(jnp.bfloat16)
    mine = pl.ds(pl.multiple_of(ex * ROWS, 16), ROWS)
    got_out[part] = send_out[mine, :]
    for n in range(1, 8):
        xl_to, y_to = (xl + n // 4) % 2, (y + n) % 4
        rows = pl.ds(pl.multiple_of((xl_to * 4 + y_to) * ROWS, 16), ROWS)
        send(send_out.at[rows], got_out.at[part], s_out, r_out, dev(z, xh, c, xl_to, y_to))

    wait_line = lines.at[pl.ds(0, 7)]
    pltpu.make_async_copy(wait_line, wait_line, s_line).wait()
    wait_slots(s_ex, 49)
    for u in range(8):
        wait_slots(s_z.at[u], 70)
        wait_slots(s_s.at[u], 32)
    wait_slots(s_d.at[0], 3)
    wait_slots(s_d.at[1], 3)
    for k in range(1, 4):
        wait_slots(s_d.at[2 * k], 6)
    for k in range(4):
        wait_slots(s_c.at[k], 224)
    seven = got_out.at[pl.ds(0, 7)]
    pltpu.make_async_copy(seven, seven, r_out).wait()
    pltpu.make_async_copy(seven, seven, s_out).wait()

    lanes = lax.broadcasted_iota(jnp.int32, (ROWS, BLK), 1) // PIECE
    for hh in range(2):
        got = [got_out[4 * hh + q].astype(jnp.float32) for q in range(4)]
        for g in range(4):
            tile = got[g]
            for q in range(4):
                if q != g:
                    tile = jnp.where(lanes == q, pltpu.roll(got[q], (q - g) * PIECE % BLK, 1), tile)
                else:
                    tile = jnp.where(lanes == q, got[q], tile)
            lo = g * 2 * BLK + hh * BLK
            out_ref[:, lo : lo + BLK] = tile.astype(jnp.bfloat16)


def on_device(tokens, gates, assign, master, owner):
    dma = pltpu.SemaphoreType.DMA
    vmem = pl.BlockSpec(memory_space=pltpu.VMEM)
    slots = master.shape[1] * lax.axis_size("rep")
    return pl.pallas_call(
        kernel,
        out_shape=jax.ShapeDtypeStruct((ROWS, FW), jnp.bfloat16),
        in_specs=[pl.BlockSpec(memory_space=pl.ANY), vmem, vmem, vmem, vmem],
        out_specs=vmem,
        scratch_shapes=[pltpu.VMEM((TOK, D), jnp.bfloat16)]
        + [pltpu.VMEM((2, slots, PIECE, BLK), jnp.bfloat16)] * 4
        + [
            pltpu.VMEM((PARTS, SLOTS, PIECE, BLK), jnp.bfloat16),
            pltpu.VMEM((16, BLK), jnp.float32),
            pltpu.VMEM((16, BLK), jnp.float32),
            pltpu.VMEM((1, 256), jnp.int32),
            pltpu.VMEM((8, 1, 256), jnp.int32),
            pltpu.SMEM((8, 1, 256), jnp.int32),
            pltpu.VMEM((8, TOK, BLK), jnp.float32),
            pltpu.VMEM((TOK, 2 * BLK), jnp.float32),
            pltpu.VMEM((TOK, BLK), jnp.float32),
            pltpu.VMEM((TOK, BLK), jnp.bfloat16),
            pltpu.VMEM((PARTS, ROWS, BLK), jnp.bfloat16),
            dma, dma,
            dma, dma,
            dma, dma((4,)),
            dma((8,)), dma((8, 4)),
            dma((8,)), dma((8,)),
            dma((8,)), dma((8, 5)),
            dma((4,)), dma((4,)),
            dma, dma,
        ],
        compiler_params=pltpu.CompilerParams(
            collective_id=0, has_side_effects=True, vmem_limit_bytes=52 * 1024 * 1024
        ),
        cost_estimate=pl.CostEstimate(
            flops=2 * TOK * D * FW, bytes_accessed=2 * TOK * D + 4 * SLOTS * BLK * 2 * BLK, transcendentals=0
        ),
        name="mixture",
    )(tokens, gates, assign, master, owner)


def solution(mesh):
    return jax.shard_map(
        on_device,
        mesh=mesh,
        in_specs=(
            P("rep", None),
            P("rep", None),
            P("rep", None),
            P("exp", "rep", None, None),
            P("exp", None),
        ),
        out_specs=P(("rep", "exp"), None),
        check_vma=False,
    )
```

```python
import functools

import jax
import jax.numpy as jnp
from jax import lax
from jax.experimental import pallas as pl
from jax.experimental.pallas import tpu as pltpu
from jax.sharding import PartitionSpec as P

D = 7168
FW = 1024
BLK = 128
SLOTS = 7
TOK = 768
HALF = TOK // 2
ROWS = 96
PARTS = 8
PIECE = 2 * BLK // PARTS
OFFSETS = (0, 1, 3, 2)
DUAL = (2, 2, 2, 2, 3, 3, 3, 7)
PANELS = 8
CHUNKS = D // (BLK * PANELS)

QUANT_LIMIT = 448.0
GRID_STEP = 16.0
MESH = pl.DeviceIdType.MESH
NT = (((1,), (1,)), ((), ()))


ORDER = (
    ("own", 0, 0), ("own", 1, 0), ("dual", 1, 0), ("own", 2, 0), ("own", 3, 0), ("own", 4, 0), ("own", 5, 0),
    ("dual", 0, 0), ("twin", 0, 0), ("hop", 1, 2), ("dual", 2, 0), ("dual", 3, 0), ("twin", 1, 0), ("dual", 4, 0),
    ("own", 6, 0), ("dual", 5, 0), ("twin", 2, 0), ("own", 7, 0), ("hop", 0, 2), ("hop", 1, 3), ("hop", 2, 2),
    ("twin", 0, 1), ("hop", 3, 2), ("hop", 4, 2), ("hop", 0, 3), ("twin", 1, 1), ("hop", 1, 4), ("hop", 2, 3),
    ("hop", 3, 3), ("twin", 0, 2), ("hop", 4, 3), ("hop", 0, 4), ("hop", 1, 5), ("hop", 5, 2), ("twin", 1, 2),
    ("hop", 2, 4), ("hop", 3, 4), ("dual", 6, 0), ("dual", 7, 0), ("twin", 3, 0), ("twin", 0, 3), ("hop", 0, 5),
    ("hop", 4, 4), ("twin", 2, 1), ("hop", 5, 3), ("hop", 2, 5), ("hop", 3, 5), ("hop", 6, 2), ("twin", 1, 3),
    ("hop", 7, 2), ("twin", 0, 4), ("hop", 4, 5), ("hop", 5, 4), ("twin", 2, 2), ("work", 0, 1), ("hop", 6, 3),
    ("work", 0, 1), ("twin", 1, 4), ("work", 0, 1), ("twin", 3, 1), ("work", 0, 1), ("hop", 7, 3), ("work", 0, 1),
    ("hop", 5, 5), ("work", 0, 1), ("twin", 2, 3), ("work", 0, 1), ("hop", 6, 4), ("twin", 3, 2), ("work", 1, 1),
    ("work", 1, 1), ("work", 1, 1), ("twin", 2, 4), ("work", 1, 1), ("hop", 7, 4), ("work", 1, 1), ("hop", 6, 5),
    ("work", 1, 1), ("twin", 3, 3), ("work", 1, 1), ("work", 2, 1), ("work", 2, 1), ("work", 2, 1), ("hop", 7, 5),
    ("twin", 3, 4), ("work", 2, 1), ("work", 2, 1), ("work", 2, 1), ("work", 2, 1),
)


def nearest_even(scaled):
    shifted = scaled * (1.0 / GRID_STEP) + 0.5
    level = jnp.floor(shifted)
    halfway = shifted == level
    odd_level = level - 2.0 * jnp.floor(level * 0.5) == 1.0
    level = jnp.where(jnp.logical_and(halfway, odd_level), level - 1.0, level)
    return level * GRID_STEP


def quantize(master_ref, peak_ref, recip_ref, pieces_ref):
    peak_ref[...] = jnp.zeros_like(peak_ref)
    for j in range(SLOTS):
        top = jnp.max(jnp.abs(master_ref[0, j]), axis=0, keepdims=True)
        for half in range(2):
            peak_ref[2 * j + half : 2 * j + half + 1, :] = top[:, half * BLK : (half + 1) * BLK]
    peak = jnp.broadcast_to(jnp.max(peak_ref[...], axis=1, keepdims=True), peak_ref.shape)
    scale = jnp.full_like(peak, 2.0**-30)
    recip = jnp.full_like(peak, 2.0**30)
    for exponent in range(-30, 1):
        exceeds = peak > QUANT_LIMIT * 2.0**exponent
        scale = jnp.where(exceeds, 2.0 ** (exponent + 1), scale)
        recip = jnp.where(exceeds, 2.0 ** (-exponent - 1), recip)
    peak_ref[...] = scale
    recip_ref[...] = recip
    for j in range(SLOTS):
        for half in range(2):
            r = 2 * j + half
            scaled = master_ref[0, j, :, half * BLK : (half + 1) * BLK] * recip_ref[r : r + 1, :]
            served = nearest_even(scaled) * peak_ref[r : r + 1, :]
            turned = served.T.astype(jnp.bfloat16)
            for q in range(PARTS // 2):
                pieces_ref[half * (PARTS // 2) + q, j] = turned[q * PIECE : (q + 1) * PIECE, :]


def slot_positions(owner):
    buckets = owner.shape[1]
    rows = lax.broadcasted_iota(jnp.int32, (buckets, buckets), 0)
    cols = lax.broadcasted_iota(jnp.int32, (buckets, buckets), 1)
    across = jnp.broadcast_to(owner, (buckets, buckets))
    down = jnp.sum(jnp.where(rows == cols, across, 0), axis=1, keepdims=True)
    earlier = jnp.logical_and(across == down, rows < cols)
    rank = jnp.sum(jnp.where(earlier, 1, 0), axis=0, keepdims=True)
    place = (owner & ~3) + ((owner & 1) << 1) + ((owner >> 1) & 1)
    return jnp.clip(place * SLOTS + rank, 0, buckets - 1)


def kernel(
    tokens_hbm, gates_hbm, assign_hbm, master_hbm, owner_hbm, out_ref,
    gates_ref, assign_ref, master_ref, owner_ref, picks, tok, w0, w1, w2, w3, placed, pieces, peak, recip, line, lines, index, gate, partial, total, send_out, got_out,
    tok_sem, idx_sem, in_sem,
    s_line, r_line, s_ex, r_ex, s_z, r_z, s_d, r_d, s_s, r_s, s_c, r_c, s_out, r_out,
):
    weights = (w0, w1, w2, w3)
    rep = lax.axis_index("rep")
    ex = lax.axis_index("exp")
    z, xh, c = rep // 4, (rep // 2) % 2, rep % 2
    xl, y = ex // 4, ex % 4
    half = (xl + xh) % 2
    part = half * 4 + y

    def dev(z_, xh_, c_, xl_, y_):
        return (z_ * 4 + xh_ * 2 + c_, xl_ * 4 + y_)

    up = dev((z + 1) % 8, xh, c, xl, y)
    down = dev((z + 7) % 8, xh, c, xl, y)
    side = dev(z, 1 - xh, c, 1 - xl, y)
    twin = dev(z, xh, 1 - c, xl, y)
    peers = [dev(z, xh, c, (xl + (n // 4)) % 2, (y + n) % 4) for n in range(1, 8)]

    inputs = [
        pltpu.make_async_copy(src, dst, in_sem.at[n])
        for n, (src, dst) in enumerate(
            ((master_hbm, master_ref), (owner_hbm, owner_ref), (gates_hbm, gates_ref), (assign_hbm, assign_ref)))
    ]
    for copy in inputs:
        copy.start()
    barrier = pltpu.get_barrier_semaphore()
    for device in [up, down, side, twin] + peers:
        pl.semaphore_signal(barrier, inc=1, device_id=device, device_id_type=MESH)

    tok_copy = pltpu.make_async_copy(tokens_hbm, tok, tok_sem)
    tok_copy.start()
    for copy in inputs:
        copy.wait()
    quantize(master_ref, peak, recip, pieces)
    pl.semaphore_wait(barrier, 11)

    def send(src, dst, s_sem, r_sem, device):
        pltpu.make_async_remote_copy(
            src_ref=src, dst_ref=dst, send_sem=s_sem, recv_sem=r_sem, device_id=device, device_id_type=MESH
        ).start()

    def wait_slots(sem, n):
        ref = w0.at[0, pl.ds(0, n)]
        pltpu.make_async_copy(ref, ref, sem).wait()

    def base(z_):
        return ((z_ % 8) * 2 + c) * 14

    own = base(z) + 7 * xh

    def at_s(u):
        return (7 + DUAL[u]) * xh

    def at_d(u):
        return (7 - DUAL[u]) * (1 - xh) + 7 * xh

    def at_d_side(u):
        return 7 * (1 - xh) + (7 - DUAL[u]) * xh

    def at_both(u):
        return (7 - DUAL[u]) * xh

    def sub(u):
        return (u + xh) % 2 if u < 2 else u % 2

    weights[0][xh, pl.ds(own, 7)] = pieces[part]
    for k in range(4):
        y_to = (y + 4 - OFFSETS[k]) % 4
        for j in range(2):
            if k == 0 and j == 1:
                continue
            xl_to = 1 - xl if k == 0 else (xl + j) % 2
            half_to = (xl_to + xh) % 2
            sub_to = (half_to + xl) % 2
            send(pieces.at[half_to * 4 + y_to], weights[k].at[sub_to, pl.ds(own, 7)], s_ex, r_ex.at[k],
                 dev(z, xh, c, xl_to, y_to))

    def ring(u, lo, n, device, h):
        w = weights[u // 2]
        ref = w.at[sub(u), pl.ds(lo, n)]
        send(ref, ref, s_z.at[u], r_z.at[u, h], device)

    def over_side(u, z_, d):
        if DUAL[u] == 7:
            return
        w = weights[u // 2]
        ref = w.at[sub(u), pl.ds(base(z_) + at_s(u), 7 - DUAL[u])]
        send(ref, ref, s_s.at[u], r_s.at[u, d], side)

    def place_line():
        line[...] = jnp.zeros_like(line)
        line[:, 0:224] = slot_positions(owner_ref[...])
        lines[xh] = line[...]
        for k in range(4):
            y_to = (y + 4 - OFFSETS[k]) % 4
            for j in range(2):
                if k == 0 and j == 1:
                    continue
                xl_to = 1 - xl if k == 0 else (xl + j) % 2
                sub_to = (xl_to + xh + xl) % 2
                send(line, lines.at[2 * k + sub_to], s_line, r_line, dev(z, xh, c, xl_to, y_to))

    def own_slots(u):
        k = u // 2
        if u == 1:
            wait_slots(r_ex.at[0], 7)
        elif u >= 2 and u % 2 == 0:
            wait_slots(r_ex.at[k], 14)
        ring(u, own, 7, up, 0)
        ring(u, own, 7, down, 0)
        ref = weights[k].at[sub(u), pl.ds(base(z) + at_d(u), DUAL[u])]
        send(ref, ref, s_d.at[u], r_d.at[u], side)
        over_side(u, z, 0)

    def dual_slots(u):
        wait_slots(r_d.at[1 - u if u < 2 else u], DUAL[u])
        ring(u, base(z) + at_d_side(u), DUAL[u], up, 0)
        ring(u, base(z) + at_d_side(u), DUAL[u], down, 0)

    def hop(u, h):
        d = h - 1
        n = 7 + DUAL[u]
        if d <= 3:
            wait_slots(r_z.at[u, d - 1], 2 * n)
            if h <= 3:
                ring(u, base(z + 8 - d) + at_both(u), n, up, d)
                ring(u, base(z + d) + at_both(u), n, down, d)
            else:
                a = max((n + 1) // 2, 7 - DUAL[u])
                one, two, from_one, from_two = up, down, base(z + 8 - d), base(z + d)
                if u % 2 == 1:
                    one, two, from_one, from_two = two, one, from_two, from_one
                ring(u, from_one + (14 - a) * xh, a, one, d)
                ring(u, from_two + a * (1 - xh) + (7 - DUAL[u]) * xh, n - a, two, d)
            over_side(u, z + 8 - d, d)
            over_side(u, z + d, d)
        else:
            wait_slots(r_z.at[u, 3], n)
            over_side(u, z + 4, 4)

    def to_twin(k, d):
        for u in (2 * k, 2 * k + 1):
            if DUAL[u] < 7:
                wait_slots(r_s.at[u, d], (7 - DUAL[u]) * (1 if d in (0, 4) else 2))
        for z_ in [z + d] if d in (0, 4) else [z + d, z + 8 - d]:
            ref = weights[k].at[:, pl.ds(base(z_), 14)]
            send(ref, ref, s_c.at[k], r_c.at[k], twin)

    def pick_gates():
        for u in range(8):
            e = ((half + u) % 2) * 4 + (y + OFFSETS[u // 2]) % 4
            pick = jnp.where(assign_ref[...] == e, gates_ref[...], 0.0)
            picks[u : u + 1, :] = jnp.sum(pick, axis=0, keepdims=True)
        turned = picks[...].T
        for u in range(8):
            gate[u] = jnp.broadcast_to(turned[:, u : u + 1], (TOK, BLK))

    def fetch_index():
        every = lines.at[pl.ds(0, 7)]
        pltpu.make_async_copy(every, every, r_line).wait()
        idx_copy = pltpu.make_async_copy(lines, index, idx_sem)
        idx_copy.start()
        idx_copy.wait()
        tok_copy.wait()

    def tiles_of(k, ch):
        w = weights[k]
        tiles = []
        for i in range(PANELS):
            bucket = (ch * PANELS + i) * 4
            tiles.append(jnp.concatenate(
                [w[s, index[2 * k + s, 0, bucket + g]] for s in range(2) for g in range(4)], axis=0))
        return jnp.concatenate(tiles, axis=1)

    def columns(ch):
        return pl.ds(pl.multiple_of(ch * (PANELS * BLK), PANELS * BLK), PANELS * BLK)

    def chunks(k, lo, hi):
        def body(ch, carry):
            partial[...] += lax.dot_general(
                tok[:, columns(ch)], tiles_of(k, ch), NT, preferred_element_type=jnp.float32)
            return carry

        if lo == 0:
            wait_slots(r_c.at[k], 224)
            partial[...] = jnp.zeros_like(partial)
        lax.fori_loop(lo, hi, body, 0)
        if hi == CHUNKS:
            term = gate[2 * k] * partial[:, 0:BLK] + gate[2 * k + 1] * partial[:, BLK : 2 * BLK]
            total[...] = term if k == 0 else total[...] + term

    def last_chunks(far):
        rows = pl.ds(pl.multiple_of(((xl + 1) % 2 if far else xl) * HALF, HALF), HALF)
        acc = partial.at[pl.ds(0, HALF)]

        def body(ch, carry):
            tiles = tiles_of(3, ch)
            placed[:, columns(ch)] = tiles
            acc[...] += lax.dot_general(
                tok[rows, columns(ch)], tiles, NT, preferred_element_type=jnp.float32)
            return carry

        if far:
            acc[...] = jnp.zeros_like(acc)
            lax.fori_loop(0, CHUNKS, body, 0)
        else:
            acc[...] = lax.dot_general(tok[rows, :], placed[...], NT, preferred_element_type=jnp.float32)
        term = gate[6, rows, :] * acc[:, 0:BLK] + gate[7, rows, :] * acc[:, BLK : 2 * BLK]
        send_out[rows, :] = (total[rows, :] + term).astype(jnp.bfloat16)
        for n in (2, 1, 3, 0):
            xl_to, y_to = (xl + 1) % 2 if far else xl, (y + n) % 4
            to = pl.ds(pl.multiple_of((xl_to * 4 + y_to) * ROWS, 16), ROWS)
            if far or n > 0:
                send(send_out.at[to], got_out.at[part], s_out, r_out, dev(z, xh, c, xl_to, y_to))
            else:
                got_out[part] = send_out[to, :]

    at = 0
    chunk = 0
    while at < len(ORDER):
        kind, u, h = ORDER[at]
        if kind == "own":
            own_slots(u)
            if u == 0:
                place_line()
        elif kind == "dual":
            dual_slots(u)
        elif kind == "hop":
            hop(u, h)
        elif kind == "twin":
            to_twin(u, h)
        else:
            n = 1
            while at + n < len(ORDER) and ORDER[at + n][:2] == ("work", u):
                n += 1
            if u == 0 and chunk == 0:
                fetch_index()
            chunks(u, chunk, chunk + n)
            chunk = (chunk + n) % CHUNKS
            at += n - 1
        if at == 8:
            pick_gates()
        at += 1

    wait_slots(r_c.at[3], 224)
    last_chunks(True)
    last_chunks(False)

    every = lines.at[pl.ds(0, 7)]
    pltpu.make_async_copy(every, every, s_line).wait()
    wait_slots(s_ex, 49)
    for u in range(8):
        wait_slots(s_z.at[u], 7 * (7 + DUAL[u]))
        wait_slots(s_d.at[u], DUAL[u])
        if DUAL[u] < 7:
            wait_slots(s_s.at[u], 8 * (7 - DUAL[u]))
    for k in range(4):
        wait_slots(s_c.at[k], 224)
    seven = got_out.at[pl.ds(0, 7)]
    pltpu.make_async_copy(seven, seven, r_out).wait()
    pltpu.make_async_copy(seven, seven, s_out).wait()

    lanes = lax.broadcasted_iota(jnp.int32, (ROWS, BLK), 1) // PIECE
    for hh in range(2):
        got = [got_out[4 * hh + q].astype(jnp.float32) for q in range(4)]
        for g in range(4):
            tile = got[g]
            for q in range(4):
                if q != g:
                    tile = jnp.where(lanes == q, pltpu.roll(got[q], (q - g) * PIECE % BLK, 1), tile)
                else:
                    tile = jnp.where(lanes == q, got[q], tile)
            lo = g * 2 * BLK + hh * BLK
            out_ref[:, lo : lo + BLK] = tile.astype(jnp.bfloat16)


def on_device(tokens, gates, assign, master, owner):
    dma = pltpu.SemaphoreType.DMA
    vmem = pl.BlockSpec(memory_space=pltpu.VMEM)
    slots = master.shape[1] * lax.axis_size("rep")
    return pl.pallas_call(
        kernel,
        out_shape=jax.ShapeDtypeStruct((ROWS, FW), jnp.bfloat16),
        in_specs=[pl.BlockSpec(memory_space=pltpu.HBM)] * 5,
        out_specs=vmem,
        scratch_shapes=[
            pltpu.VMEM((8, TOK), jnp.float32),
            pltpu.VMEM((8, TOK), jnp.int32),
            pltpu.VMEM(master.shape, jnp.float32),
            pltpu.VMEM(owner.shape, jnp.int32),
            pltpu.VMEM((8, TOK), jnp.float32),
            pltpu.VMEM((TOK, D), jnp.bfloat16),
        ]
        + [pltpu.VMEM((2, slots, PIECE, BLK), jnp.bfloat16)] * 4
        + [
            pltpu.VMEM((2 * BLK, D), jnp.bfloat16),
            pltpu.VMEM((PARTS, SLOTS, PIECE, BLK), jnp.bfloat16),
            pltpu.VMEM((16, BLK), jnp.float32),
            pltpu.VMEM((16, BLK), jnp.float32),
            pltpu.VMEM((1, 256), jnp.int32),
            pltpu.VMEM((8, 1, 256), jnp.int32),
            pltpu.SMEM((8, 1, 256), jnp.int32),
            pltpu.VMEM((8, TOK, BLK), jnp.float32),
            pltpu.VMEM((TOK, 2 * BLK), jnp.float32),
            pltpu.VMEM((TOK, BLK), jnp.float32),
            pltpu.VMEM((TOK, BLK), jnp.bfloat16),
            pltpu.VMEM((PARTS, ROWS, BLK), jnp.bfloat16),
            dma, dma, dma((4,)),
            dma, dma,
            dma, dma((4,)),
            dma((8,)), dma((8, 4)),
            dma((8,)), dma((8,)),
            dma((8,)), dma((8, 5)),
            dma((4,)), dma((4,)),
            dma, dma,
        ],
        compiler_params=pltpu.CompilerParams(
            collective_id=0, has_side_effects=True, vmem_limit_bytes=54 * 1024 * 1024
        ),
        cost_estimate=pl.CostEstimate(
            flops=2 * TOK * D * FW, bytes_accessed=2 * TOK * D + 4 * SLOTS * BLK * 2 * BLK, transcendentals=0
        ),
        name="mixture",
    )(tokens, gates.T, assign.T, master, owner)


def solution(mesh):
    return jax.shard_map(
        on_device,
        mesh=mesh,
        in_specs=(
            P("rep", None),
            P("rep", None),
            P("rep", None),
            P("exp", "rep", None, None),
            P("exp", None),
        ),
        out_specs=P(("rep", "exp"), None),
        check_vma=False,
    )
```

```python
import functools

import jax
import jax.numpy as jnp
from jax import lax
from jax.experimental import pallas as pl
from jax.experimental.pallas import tpu as pltpu
from jax.sharding import PartitionSpec as P

D = 7168
FW = 1024
BLK = 128
SLOTS = 7
TOK = 768
HALF = TOK // 2
ROWS = 96
PARTS = 8
PIECE = 2 * BLK // PARTS
OFFSETS = (0, 1, 3, 2)
DUAL = (2, 2, 2, 2, 2, 2, 7, 7)
PANELS = 8
CHUNKS = D // (BLK * PANELS)

QUANT_LIMIT = 448.0
GRID_STEP = 16.0
MESH = pl.DeviceIdType.MESH
NT = (((1,), (1,)), ((), ()))


ORDER = (
    ("own", 0, 0), ("own", 1, 0), ("own", 2, 0), ("dual", 1, 0), ("own", 3, 0), ("own", 4, 0), ("dual", 0, 0),
    ("own", 5, 0), ("dual", 2, 0), ("hop", 1, 2), ("own", 6, 0), ("dual", 3, 0), ("hop", 0, 2), ("hop", 2, 2),
    ("hop", 1, 3), ("own", 7, 0), ("dual", 5, 0), ("hop", 3, 2), ("twin", 1, 0), ("hop", 0, 3), ("hop", 2, 3),
    ("dual", 4, 0), ("hop", 1, 4), ("hop", 3, 3), ("hop", 0, 4), ("hop", 5, 2), ("twin", 2, 0), ("dual", 6, 0),
    ("hop", 1, 5), ("hop", 2, 4), ("twin", 0, 2), ("twin", 0, 1), ("hop", 0, 5), ("hop", 3, 4), ("hop", 4, 2),
    ("hop", 5, 3), ("dual", 7, 0), ("twin", 0, 3), ("hop", 3, 5), ("twin", 0, 0), ("twin", 1, 1), ("hop", 2, 5),
    ("hop", 4, 3), ("twin", 0, 4), ("hop", 5, 4), ("hop", 6, 2), ("hop", 4, 4), ("twin", 1, 2), ("hop", 7, 2),
    ("work", 0, 1), ("hop", 5, 5), ("work", 0, 1), ("twin", 1, 3), ("work", 0, 1), ("twin", 1, 4), ("twin", 3, 0),
    ("work", 0, 1), ("hop", 6, 3), ("twin", 2, 1), ("hop", 4, 5), ("twin", 3, 1), ("work", 0, 1), ("work", 0, 1),
    ("twin", 2, 2), ("work", 0, 1), ("hop", 7, 3), ("work", 1, 1), ("work", 1, 1), ("twin", 2, 3), ("work", 1, 1),
    ("work", 1, 1), ("twin", 2, 4), ("hop", 6, 4), ("work", 1, 1), ("work", 1, 1), ("work", 1, 1), ("hop", 7, 4),
    ("twin", 3, 3), ("twin", 3, 2), ("work", 2, 1), ("work", 2, 1), ("hop", 6, 5), ("twin", 3, 4), ("work", 2, 1),
    ("work", 2, 1), ("work", 2, 1), ("hop", 7, 5), ("work", 2, 1), ("work", 2, 1),
)


def nearest_even(scaled):
    shifted = scaled * (1.0 / GRID_STEP) + 0.5
    level = jnp.floor(shifted)
    halfway = shifted == level
    odd_level = level - 2.0 * jnp.floor(level * 0.5) == 1.0
    level = jnp.where(jnp.logical_and(halfway, odd_level), level - 1.0, level)
    return level * GRID_STEP


def quantize(master_ref, peak_ref, recip_ref, pieces_ref):
    peak_ref[...] = jnp.zeros_like(peak_ref)
    for j in range(SLOTS):
        top = jnp.max(jnp.abs(master_ref[0, j]), axis=0, keepdims=True)
        for half in range(2):
            peak_ref[2 * j + half : 2 * j + half + 1, :] = top[:, half * BLK : (half + 1) * BLK]
    peak = jnp.broadcast_to(jnp.max(peak_ref[...], axis=1, keepdims=True), peak_ref.shape)
    scale = jnp.full_like(peak, 2.0**-30)
    recip = jnp.full_like(peak, 2.0**30)
    for exponent in range(-30, 1):
        exceeds = peak > QUANT_LIMIT * 2.0**exponent
        scale = jnp.where(exceeds, 2.0 ** (exponent + 1), scale)
        recip = jnp.where(exceeds, 2.0 ** (-exponent - 1), recip)
    peak_ref[...] = scale
    recip_ref[...] = recip
    for j in range(SLOTS):
        for half in range(2):
            r = 2 * j + half
            scaled = master_ref[0, j, :, half * BLK : (half + 1) * BLK] * recip_ref[r : r + 1, :]
            served = nearest_even(scaled) * peak_ref[r : r + 1, :]
            turned = served.T.astype(jnp.bfloat16)
            for q in range(PARTS // 2):
                pieces_ref[half * (PARTS // 2) + q, j] = turned[q * PIECE : (q + 1) * PIECE, :]


def slot_positions(owner):
    buckets = owner.shape[1]
    rows = lax.broadcasted_iota(jnp.int32, (buckets, buckets), 0)
    cols = lax.broadcasted_iota(jnp.int32, (buckets, buckets), 1)
    across = jnp.broadcast_to(owner, (buckets, buckets))
    down = jnp.sum(jnp.where(rows == cols, across, 0), axis=1, keepdims=True)
    earlier = jnp.logical_and(across == down, rows < cols)
    rank = jnp.sum(jnp.where(earlier, 1, 0), axis=0, keepdims=True)
    place = (owner & ~3) + ((owner & 1) << 1) + ((owner >> 1) & 1)
    return jnp.clip(place * SLOTS + rank, 0, buckets - 1)


def kernel(
    tokens_hbm, gates_hbm, assign_hbm, master_hbm, owner_hbm, out_ref,
    gates_ref, assign_ref, master_ref, owner_ref, picks, tok, w0, w1, w2, w3, placed, pieces, peak, recip, line, lines, index, gate, partial, total, send_out, got_out,
    tok_sem, idx_sem, in_sem,
    s_line, r_line, s_ex, r_ex, s_z, r_z, s_d, r_d, s_s, r_s, s_c, r_c, s_out, r_out,
):
    weights = (w0, w1, w2, w3)
    rep = lax.axis_index("rep")
    ex = lax.axis_index("exp")
    z, xh, c = rep // 4, (rep // 2) % 2, rep % 2
    xl, y = ex // 4, ex % 4
    half = (xl + xh) % 2
    part = half * 4 + y

    def dev(z_, xh_, c_, xl_, y_):
        return (z_ * 4 + xh_ * 2 + c_, xl_ * 4 + y_)

    up = dev((z + 1) % 8, xh, c, xl, y)
    down = dev((z + 7) % 8, xh, c, xl, y)
    side = dev(z, 1 - xh, c, 1 - xl, y)
    twin = dev(z, xh, 1 - c, xl, y)
    up_twin = dev((z + 1) % 8, xh, 1 - c, xl, y)
    down_twin = dev((z + 7) % 8, xh, 1 - c, xl, y)
    peers = [dev(z, xh, c, (xl + (n // 4)) % 2, (y + n) % 4) for n in range(1, 8)]

    inputs = [
        pltpu.make_async_copy(src, dst, in_sem.at[n])
        for n, (src, dst) in enumerate(
            ((master_hbm, master_ref), (owner_hbm, owner_ref), (gates_hbm, gates_ref), (assign_hbm, assign_ref)))
    ]
    for copy in inputs:
        copy.start()
    barrier = pltpu.get_barrier_semaphore()
    for device in [up, down, side, twin, up_twin, down_twin] + peers:
        pl.semaphore_signal(barrier, inc=1, device_id=device, device_id_type=MESH)

    tok_copy = pltpu.make_async_copy(tokens_hbm, tok, tok_sem)
    tok_copy.start()
    for copy in inputs:
        copy.wait()
    quantize(master_ref, peak, recip, pieces)
    pl.semaphore_wait(barrier, 13)

    def send(src, dst, s_sem, r_sem, device):
        pltpu.make_async_remote_copy(
            src_ref=src, dst_ref=dst, send_sem=s_sem, recv_sem=r_sem, device_id=device, device_id_type=MESH
        ).start()

    def wait_slots(sem, n):
        ref = w0.at[0, pl.ds(0, n)]
        pltpu.make_async_copy(ref, ref, sem).wait()

    def base(z_):
        return ((z_ % 8) * 2 + c) * 14

    own = base(z) + 7 * xh

    def at_s(u):
        return (7 + DUAL[u]) * xh

    def at_d(u):
        return (7 - DUAL[u]) * (1 - xh) + 7 * xh

    def at_d_side(u):
        return 7 * (1 - xh) + (7 - DUAL[u]) * xh

    def at_both(u):
        return (7 - DUAL[u]) * xh

    def sub(u):
        return (u + xh) % 2 if u < 2 else u % 2

    weights[0][xh, pl.ds(own, 7)] = pieces[part]
    for k in range(4):
        y_to = (y + 4 - OFFSETS[k]) % 4
        for j in range(2):
            if k == 0 and j == 1:
                continue
            xl_to = 1 - xl if k == 0 else (xl + j) % 2
            half_to = (xl_to + xh) % 2
            sub_to = (half_to + xl) % 2
            send(pieces.at[half_to * 4 + y_to], weights[k].at[sub_to, pl.ds(own, 7)], s_ex, r_ex.at[k],
                 dev(z, xh, c, xl_to, y_to))

    def ring(u, lo, n, device, h):
        w = weights[u // 2]
        ref = w.at[sub(u), pl.ds(lo, n)]
        send(ref, ref, s_z.at[u], r_z.at[u, h], device)

    def over_side(u, z_, d):
        if DUAL[u] == 7:
            return
        w = weights[u // 2]
        ref = w.at[sub(u), pl.ds(base(z_) + at_s(u), 7 - DUAL[u])]
        send(ref, ref, s_s.at[u], r_s.at[u, d], side)

    def place_line():
        line[...] = jnp.zeros_like(line)
        line[:, 0:224] = slot_positions(owner_ref[...])
        lines[xh] = line[...]
        for k in range(4):
            y_to = (y + 4 - OFFSETS[k]) % 4
            for j in range(2):
                if k == 0 and j == 1:
                    continue
                xl_to = 1 - xl if k == 0 else (xl + j) % 2
                sub_to = (xl_to + xh + xl) % 2
                send(line, lines.at[2 * k + sub_to], s_line, r_line, dev(z, xh, c, xl_to, y_to))

    def own_slots(u):
        k = u // 2
        if u == 1:
            wait_slots(r_ex.at[0], 7)
        elif u >= 2 and u % 2 == 0:
            wait_slots(r_ex.at[k], 14)
        ring(u, own, 7, up, 0)
        ring(u, own, 7, down, 0)
        ref = weights[k].at[sub(u), pl.ds(base(z) + at_d(u), DUAL[u])]
        send(ref, ref, s_d.at[u], r_d.at[u], side)
        over_side(u, z, 0)

    def dual_slots(u):
        wait_slots(r_d.at[1 - u if u < 2 else u], DUAL[u])
        ring(u, base(z) + at_d_side(u), DUAL[u], up, 0)
        ring(u, base(z) + at_d_side(u), DUAL[u], down, 0)

    def hop(u, h):
        d = h - 1
        n = 7 + DUAL[u]
        if d <= 3:
            wait_slots(r_z.at[u, d - 1], 2 * n)
            if h <= 3:
                ring(u, base(z + 8 - d) + at_both(u), n, up, d)
                ring(u, base(z + d) + at_both(u), n, down, d)
            else:
                a = max((n + 1) // 2, 7 - DUAL[u])
                one, two, from_one, from_two = up, down, base(z + 8 - d), base(z + d)
                if u % 2 == 1:
                    one, two, from_one, from_two = two, one, from_two, from_one
                ring(u, from_one + (14 - a) * xh, a, one, d)
                ring(u, from_two + a * (1 - xh) + (7 - DUAL[u]) * xh, n - a, two, d)
                if u == 7:
                    for lo, m, device in (
                        (from_one + (14 - a) * xh, a, (down_twin)),
                        (from_two + a * (1 - xh) + (7 - DUAL[u]) * xh, n - a, (up_twin)),
                    ):
                        ref = weights[3].at[1, pl.ds(lo, m)]
                        send(ref, ref, s_c.at[3], r_c.at[3], device)
            over_side(u, z + 8 - d, d)
            over_side(u, z + d, d)
        else:
            wait_slots(r_z.at[u, 3], n)
            over_side(u, z + 4, 4)

    def to_twin(k, d):
        last = (k, d) == (3, 4)
        for u in (2 * k, 2 * k + 1):
            if DUAL[u] < 7:
                wait_slots(r_s.at[u, d], (7 - DUAL[u]) * (1 if d in (0, 4) else 2))
        for z_ in [z + d] if d in (0, 4) else [z + d, z + 8 - d]:
            ref = weights[k].at[pl.ds(0, 1 if last else 2), pl.ds(base(z_), 14)]
            send(ref, ref, s_c.at[k], r_c.at[k], twin)

    def pick_gates():
        for u in range(8):
            e = ((half + u) % 2) * 4 + (y + OFFSETS[u // 2]) % 4
            pick = jnp.where(assign_ref[...] == e, gates_ref[...], 0.0)
            picks[u : u + 1, :] = jnp.sum(pick, axis=0, keepdims=True)
        turned = picks[...].T
        for u in range(8):
            gate[u] = jnp.broadcast_to(turned[:, u : u + 1], (TOK, BLK))

    idx_copy = pltpu.make_async_copy(lines, index, idx_sem)

    def fetch_index():
        every = lines.at[pl.ds(0, 7)]
        pltpu.make_async_copy(every, every, r_line).wait()
        idx_copy.start()

    def tiles_of(k, ch):
        w = weights[k]
        tiles = []
        for i in range(PANELS):
            bucket = (ch * PANELS + i) * 4
            tiles.append(jnp.concatenate(
                [w[s, index[2 * k + s, 0, bucket + g]] for s in range(2) for g in range(4)], axis=0))
        return jnp.concatenate(tiles, axis=1)

    def columns(ch):
        return pl.ds(pl.multiple_of(ch * (PANELS * BLK), PANELS * BLK), PANELS * BLK)

    def step(kind, u, h):
        if kind == "own":
            own_slots(u)
            if u == 0:
                place_line()
        elif kind == "dual":
            dual_slots(u)
        elif kind == "hop":
            hop(u, h)
        else:
            to_twin(u, h)

    def chunks(k, between, fresh):
        wait_slots(r_c.at[k], 224)
        partial[...] = jnp.zeros_like(partial)

        def body(ch, carry):
            partial[...] += lax.dot_general(
                tok[:, columns(ch)], tiles_of(k, ch), NT, preferred_element_type=jnp.float32)
            for n, steps in enumerate(between):
                if steps:
                    @pl.when(ch == n)
                    def _():
                        for each in steps:
                            step(*each)
            return carry

        lax.fori_loop(0, CHUNKS, body, 0)
        term = gate[2 * k] * partial[:, 0:BLK] + gate[2 * k + 1] * partial[:, BLK : 2 * BLK]
        total[...] = term if fresh else total[...] + term

    def last_chunks(far):
        rows = pl.ds(pl.multiple_of(((xl + 1) % 2 if far else xl) * HALF, HALF), HALF)
        acc = partial.at[pl.ds(0, HALF)]

        def body(ch, carry):
            tiles = tiles_of(3, ch)
            placed[:, columns(ch)] = tiles
            acc[...] += lax.dot_general(
                tok[rows, columns(ch)], tiles, NT, preferred_element_type=jnp.float32)
            return carry

        if far:
            acc[...] = jnp.zeros_like(acc)
            lax.fori_loop(0, CHUNKS, body, 0)
        else:
            acc[...] = lax.dot_general(tok[rows, :], placed[...], NT, preferred_element_type=jnp.float32)
        term = gate[6, rows, :] * acc[:, 0:BLK] + gate[7, rows, :] * acc[:, BLK : 2 * BLK]
        send_out[rows, :] = (total[rows, :] + term).astype(jnp.bfloat16)
        for n in (2, 1, 3, 0):
            xl_to, y_to = (xl + 1) % 2 if far else xl, (y + n) % 4
            to = pl.ds(pl.multiple_of((xl_to * 4 + y_to) * ROWS, 16), ROWS)
            if far or n > 0:
                send(send_out.at[to], got_out.at[part], s_out, r_out, dev(z, xh, c, xl_to, y_to))
            else:
                got_out[part] = send_out[to, :]

    first = [n for n, each in enumerate(ORDER) if each[0] == "work"]
    for n, each in enumerate(ORDER[: first[0]]):
        step(*each)
        if n == 8:
            pick_gates()
        elif n == 14:
            fetch_index()
    idx_copy.wait()
    tok_copy.wait()
    ends = first[1:] + [len(ORDER)]
    for n in range(0, 3 * CHUNKS, CHUNKS):
        between = [ORDER[lo + 1 : hi] for lo, hi in zip(first[n : n + CHUNKS], ends[n:])]
        chunks(ORDER[first[n]][1], between, n == 0)

    wait_slots(r_c.at[3], 224)
    last_chunks(True)
    last_chunks(False)

    every = lines.at[pl.ds(0, 7)]
    pltpu.make_async_copy(every, every, s_line).wait()
    wait_slots(s_ex, 49)
    for u in range(8):
        wait_slots(s_z.at[u], 7 * (7 + DUAL[u]))
        wait_slots(s_d.at[u], DUAL[u])
        if DUAL[u] < 7:
            wait_slots(s_s.at[u], 8 * (7 - DUAL[u]))
    for k in range(4):
        wait_slots(s_c.at[k], 224)
    seven = got_out.at[pl.ds(0, 7)]
    pltpu.make_async_copy(seven, seven, r_out).wait()
    pltpu.make_async_copy(seven, seven, s_out).wait()

    lanes = lax.broadcasted_iota(jnp.int32, (ROWS, BLK), 1) // PIECE
    for hh in range(2):
        got = [got_out[4 * hh + q].astype(jnp.float32) for q in range(4)]
        for g in range(4):
            tile = got[g]
            for q in range(4):
                if q != g:
                    tile = jnp.where(lanes == q, pltpu.roll(got[q], (q - g) * PIECE % BLK, 1), tile)
                else:
                    tile = jnp.where(lanes == q, got[q], tile)
            lo = g * 2 * BLK + hh * BLK
            out_ref[:, lo : lo + BLK] = tile.astype(jnp.bfloat16)


def on_device(tokens, gates, assign, master, owner):
    dma = pltpu.SemaphoreType.DMA
    vmem = pl.BlockSpec(memory_space=pltpu.VMEM)
    slots = master.shape[1] * lax.axis_size("rep")
    return pl.pallas_call(
        kernel,
        out_shape=jax.ShapeDtypeStruct((ROWS, FW), jnp.bfloat16),
        in_specs=[pl.BlockSpec(memory_space=pltpu.HBM)] * 5,
        out_specs=vmem,
        scratch_shapes=[
            pltpu.VMEM((8, TOK), jnp.float32),
            pltpu.VMEM((8, TOK), jnp.int32),
            pltpu.VMEM(master.shape, jnp.float32),
            pltpu.VMEM(owner.shape, jnp.int32),
            pltpu.VMEM((8, TOK), jnp.float32),
            pltpu.VMEM((TOK, D), jnp.bfloat16),
        ]
        + [pltpu.VMEM((2, slots, PIECE, BLK), jnp.bfloat16)] * 4
        + [
            pltpu.VMEM((2 * BLK, D), jnp.bfloat16),
            pltpu.VMEM((PARTS, SLOTS, PIECE, BLK), jnp.bfloat16),
            pltpu.VMEM((16, BLK), jnp.float32),
            pltpu.VMEM((16, BLK), jnp.float32),
            pltpu.VMEM((1, 256), jnp.int32),
            pltpu.VMEM((8, 1, 256), jnp.int32),
            pltpu.SMEM((8, 1, 256), jnp.int32),
            pltpu.VMEM((8, TOK, BLK), jnp.float32),
            pltpu.VMEM((TOK, 2 * BLK), jnp.float32),
            pltpu.VMEM((TOK, BLK), jnp.float32),
            pltpu.VMEM((TOK, BLK), jnp.bfloat16),
            pltpu.VMEM((PARTS, ROWS, BLK), jnp.bfloat16),
            dma, dma, dma((4,)),
            dma, dma,
            dma, dma((4,)),
            dma((8,)), dma((8, 4)),
            dma((8,)), dma((8,)),
            dma((8,)), dma((8, 5)),
            dma((4,)), dma((4,)),
            dma, dma,
        ],
        compiler_params=pltpu.CompilerParams(
            collective_id=0, has_side_effects=True, vmem_limit_bytes=54 * 1024 * 1024
        ),
        cost_estimate=pl.CostEstimate(
            flops=2 * TOK * D * FW, bytes_accessed=2 * TOK * D + 4 * SLOTS * BLK * 2 * BLK, transcendentals=0
        ),
        name="mixture",
    )(tokens, gates.T, assign.T, master, owner)


def solution(mesh):
    return jax.shard_map(
        on_device,
        mesh=mesh,
        in_specs=(
            P("rep", None),
            P("rep", None),
            P("rep", None),
            P("exp", "rep", None, None),
            P("exp", None),
        ),
        out_specs=P(("rep", "exp"), None),
        check_vma=False,
    )
```

```python
import functools

import jax
import jax.numpy as jnp
from jax import lax
from jax.experimental import pallas as pl
from jax.experimental.pallas import tpu as pltpu
from jax.sharding import PartitionSpec as P

D = 7168
FW = 1024
BLK = 128
SLOTS = 7
TOK = 768
HALF = TOK // 2
ROWS = 96
PARTS = 8
PIECE = 2 * BLK // PARTS
OFFSETS = (0, 1, 3, 2)
DUAL = (2, 2, 2, 2, 2, 2, 7, 7)
PANELS = 8
LAST_PANELS = 14
CHUNKS = D // (BLK * PANELS)

QUANT_LIMIT = 448.0
GRID_STEP = 16.0
MESH = pl.DeviceIdType.MESH
NT = (((1,), (1,)), ((), ()))


ORDER = (
    ("own", 0, 0), ("own", 1, 0), ("own", 2, 0), ("dual", 1, 0), ("own", 3, 0), ("own", 4, 0), ("dual", 0, 0),
    ("own", 5, 0), ("dual", 2, 0), ("hop", 1, 2), ("own", 6, 0), ("dual", 3, 0), ("hop", 0, 2), ("hop", 2, 2),
    ("hop", 1, 3), ("own", 7, 0), ("dual", 5, 0), ("hop", 3, 2), ("twin", 1, 0), ("hop", 0, 3), ("hop", 2, 3),
    ("dual", 4, 0), ("hop", 1, 4), ("hop", 3, 3), ("hop", 0, 4), ("hop", 5, 2), ("twin", 2, 0), ("dual", 6, 0),
    ("hop", 1, 5), ("hop", 2, 4), ("twin", 0, 2), ("twin", 0, 1), ("hop", 0, 5), ("hop", 3, 4), ("hop", 4, 2),
    ("hop", 5, 3), ("dual", 7, 0), ("twin", 0, 3), ("hop", 3, 5), ("twin", 0, 0), ("twin", 1, 1), ("hop", 2, 5),
    ("hop", 4, 3), ("twin", 0, 4), ("hop", 5, 4), ("hop", 6, 2), ("hop", 4, 4), ("twin", 1, 2), ("hop", 7, 2),
    ("work", 0, 1), ("hop", 5, 5), ("work", 0, 1), ("twin", 1, 3), ("work", 0, 1), ("twin", 1, 4), ("twin", 3, 0),
    ("work", 0, 1), ("hop", 6, 3), ("twin", 2, 1), ("hop", 4, 5), ("twin", 3, 1), ("work", 0, 1), ("work", 0, 1),
    ("twin", 2, 2), ("work", 0, 1), ("hop", 7, 3), ("work", 1, 1), ("work", 1, 1), ("twin", 2, 3), ("work", 1, 1),
    ("work", 1, 1), ("twin", 2, 4), ("hop", 6, 4), ("work", 1, 1), ("work", 1, 1), ("work", 1, 1), ("hop", 7, 4),
    ("twin", 3, 3), ("twin", 3, 2), ("work", 2, 1), ("work", 2, 1), ("hop", 6, 5), ("twin", 3, 4), ("work", 2, 1),
    ("work", 2, 1), ("work", 2, 1), ("hop", 7, 5), ("work", 2, 1), ("work", 2, 1),
)


def nearest_even(scaled):
    shifted = scaled * (1.0 / GRID_STEP) + 0.5
    level = jnp.floor(shifted)
    halfway = shifted == level
    odd_level = level - 2.0 * jnp.floor(level * 0.5) == 1.0
    level = jnp.where(jnp.logical_and(halfway, odd_level), level - 1.0, level)
    return level * GRID_STEP


def quantize(master_ref, peak_ref, recip_ref, pieces_ref):
    peak_ref[...] = jnp.zeros_like(peak_ref)
    for j in range(SLOTS):
        top = jnp.max(jnp.abs(master_ref[0, j]), axis=0, keepdims=True)
        for half in range(2):
            peak_ref[2 * j + half : 2 * j + half + 1, :] = top[:, half * BLK : (half + 1) * BLK]
    peak = jnp.broadcast_to(jnp.max(peak_ref[...], axis=1, keepdims=True), peak_ref.shape)
    scale = jnp.full_like(peak, 2.0**-30)
    recip = jnp.full_like(peak, 2.0**30)
    for exponent in range(-30, 1):
        exceeds = peak > QUANT_LIMIT * 2.0**exponent
        scale = jnp.where(exceeds, 2.0 ** (exponent + 1), scale)
        recip = jnp.where(exceeds, 2.0 ** (-exponent - 1), recip)
    peak_ref[...] = scale
    recip_ref[...] = recip
    for j in range(SLOTS):
        for half in range(2):
            r = 2 * j + half
            scaled = master_ref[0, j, :, half * BLK : (half + 1) * BLK] * recip_ref[r : r + 1, :]
            served = nearest_even(scaled) * peak_ref[r : r + 1, :]
            turned = served.T.astype(jnp.bfloat16)
            for q in range(PARTS // 2):
                pieces_ref[half * (PARTS // 2) + q, j] = turned[q * PIECE : (q + 1) * PIECE, :]


def slot_positions(owner):
    buckets = owner.shape[1]
    rows = lax.broadcasted_iota(jnp.int32, (buckets, buckets), 0)
    cols = lax.broadcasted_iota(jnp.int32, (buckets, buckets), 1)
    across = jnp.broadcast_to(owner, (buckets, buckets))
    down = jnp.sum(jnp.where(rows == cols, across, 0), axis=1, keepdims=True)
    earlier = jnp.logical_and(across == down, rows < cols)
    rank = jnp.sum(jnp.where(earlier, 1, 0), axis=0, keepdims=True)
    place = (owner & ~3) + ((owner & 1) << 1) + ((owner >> 1) & 1)
    return jnp.clip(place * SLOTS + rank, 0, buckets - 1)


def kernel(
    tokens_hbm, gates_hbm, assign_hbm, master_hbm, owner_hbm, out_ref,
    gates_ref, assign_ref, master_ref, owner_ref, picks, tok, w0, w1, w2, w3, placed, pieces, peak, recip, line, lines, index, gate, partial, total, send_out, got_out,
    tok_sem, idx_sem, in_sem,
    s_line, r_line, s_ex, r_ex, s_z, r_z, s_d, r_d, s_s, r_s, s_c, r_c, s_out, r_out,
):
    weights = (w0, w1, w2, w3)
    rep = lax.axis_index("rep")
    ex = lax.axis_index("exp")
    z, xh, c = rep // 4, (rep // 2) % 2, rep % 2
    xl, y = ex // 4, ex % 4
    half = (xl + xh) % 2
    part = half * 4 + y

    def dev(z_, xh_, c_, xl_, y_):
        return (z_ * 4 + xh_ * 2 + c_, xl_ * 4 + y_)

    up = dev((z + 1) % 8, xh, c, xl, y)
    down = dev((z + 7) % 8, xh, c, xl, y)
    side = dev(z, 1 - xh, c, 1 - xl, y)
    twin = dev(z, xh, 1 - c, xl, y)
    up_twin = dev((z + 1) % 8, xh, 1 - c, xl, y)
    down_twin = dev((z + 7) % 8, xh, 1 - c, xl, y)
    peers = [dev(z, xh, c, (xl + (n // 4)) % 2, (y + n) % 4) for n in range(1, 8)]

    inputs = [
        pltpu.make_async_copy(src, dst, in_sem.at[n])
        for n, (src, dst) in enumerate(
            ((master_hbm, master_ref), (owner_hbm, owner_ref), (gates_hbm, gates_ref), (assign_hbm, assign_ref)))
    ]
    for copy in inputs:
        copy.start()
    barrier = pltpu.get_barrier_semaphore()
    for device in [up, down, side, twin, up_twin, down_twin] + peers:
        pl.semaphore_signal(barrier, inc=1, device_id=device, device_id_type=MESH)

    tok_copy = pltpu.make_async_copy(tokens_hbm, tok, tok_sem)
    tok_copy.start()
    for copy in inputs:
        copy.wait()
    quantize(master_ref, peak, recip, pieces)
    pl.semaphore_wait(barrier, 13)

    def send(src, dst, s_sem, r_sem, device):
        pltpu.make_async_remote_copy(
            src_ref=src, dst_ref=dst, send_sem=s_sem, recv_sem=r_sem, device_id=device, device_id_type=MESH
        ).start()

    def wait_slots(sem, n):
        ref = w0.at[0, pl.ds(0, n)]
        pltpu.make_async_copy(ref, ref, sem).wait()

    def base(z_):
        return ((z_ % 8) * 2 + c) * 14

    own = base(z) + 7 * xh

    def at_s(u):
        return (7 + DUAL[u]) * xh

    def at_d(u):
        return (7 - DUAL[u]) * (1 - xh) + 7 * xh

    def at_d_side(u):
        return 7 * (1 - xh) + (7 - DUAL[u]) * xh

    def at_both(u):
        return (7 - DUAL[u]) * xh

    def sub(u):
        return (u + xh) % 2 if u < 2 else u % 2

    weights[0][xh, pl.ds(own, 7)] = pieces[part]
    for k in range(4):
        y_to = (y + 4 - OFFSETS[k]) % 4
        for j in range(2):
            if k == 0 and j == 1:
                continue
            xl_to = 1 - xl if k == 0 else (xl + j) % 2
            half_to = (xl_to + xh) % 2
            sub_to = (half_to + xl) % 2
            send(pieces.at[half_to * 4 + y_to], weights[k].at[sub_to, pl.ds(own, 7)], s_ex, r_ex.at[k],
                 dev(z, xh, c, xl_to, y_to))

    def ring(u, lo, n, device, h):
        w = weights[u // 2]
        ref = w.at[sub(u), pl.ds(lo, n)]
        send(ref, ref, s_z.at[u], r_z.at[u, h], device)

    def over_side(u, z_, d):
        if DUAL[u] == 7:
            return
        w = weights[u // 2]
        ref = w.at[sub(u), pl.ds(base(z_) + at_s(u), 7 - DUAL[u])]
        send(ref, ref, s_s.at[u], r_s.at[u, d], side)

    def place_line():
        line[...] = jnp.zeros_like(line)
        line[:, 0:224] = slot_positions(owner_ref[...])
        lines[xh] = line[...]
        for k in range(4):
            y_to = (y + 4 - OFFSETS[k]) % 4
            for j in range(2):
                if k == 0 and j == 1:
                    continue
                xl_to = 1 - xl if k == 0 else (xl + j) % 2
                sub_to = (xl_to + xh + xl) % 2
                send(line, lines.at[2 * k + sub_to], s_line, r_line, dev(z, xh, c, xl_to, y_to))

    def own_slots(u):
        k = u // 2
        if u == 1:
            wait_slots(r_ex.at[0], 7)
        elif u >= 2 and u % 2 == 0:
            wait_slots(r_ex.at[k], 14)
        ring(u, own, 7, up, 0)
        ring(u, own, 7, down, 0)
        ref = weights[k].at[sub(u), pl.ds(base(z) + at_d(u), DUAL[u])]
        send(ref, ref, s_d.at[u], r_d.at[u], side)
        over_side(u, z, 0)

    def dual_slots(u):
        wait_slots(r_d.at[1 - u if u < 2 else u], DUAL[u])
        ring(u, base(z) + at_d_side(u), DUAL[u], up, 0)
        ring(u, base(z) + at_d_side(u), DUAL[u], down, 0)

    def hop(u, h):
        d = h - 1
        n = 7 + DUAL[u]
        if d <= 3:
            wait_slots(r_z.at[u, d - 1], 2 * n)
            if h <= 3:
                ring(u, base(z + 8 - d) + at_both(u), n, up, d)
                ring(u, base(z + d) + at_both(u), n, down, d)
            else:
                a = max((n + 1) // 2, 7 - DUAL[u])
                one, two, from_one, from_two = up, down, base(z + 8 - d), base(z + d)
                if u % 2 == 1:
                    one, two, from_one, from_two = two, one, from_two, from_one
                ring(u, from_one + (14 - a) * xh, a, one, d)
                ring(u, from_two + a * (1 - xh) + (7 - DUAL[u]) * xh, n - a, two, d)
                if u == 7:
                    for lo, m, device in (
                        (from_one + (14 - a) * xh, a, (down_twin)),
                        (from_two + a * (1 - xh) + (7 - DUAL[u]) * xh, n - a, (up_twin)),
                    ):
                        ref = weights[3].at[1, pl.ds(lo, m)]
                        send(ref, ref, s_c.at[3], r_c.at[3], device)
            over_side(u, z + 8 - d, d)
            over_side(u, z + d, d)
        else:
            wait_slots(r_z.at[u, 3], n)
            over_side(u, z + 4, 4)

    def to_twin(k, d):
        last = (k, d) == (3, 4)
        for u in (2 * k, 2 * k + 1):
            if DUAL[u] < 7:
                wait_slots(r_s.at[u, d], (7 - DUAL[u]) * (1 if d in (0, 4) else 2))
        for z_ in [z + d] if d in (0, 4) else [z + d, z + 8 - d]:
            ref = weights[k].at[pl.ds(0, 1 if last else 2), pl.ds(base(z_), 14)]
            send(ref, ref, s_c.at[k], r_c.at[k], twin)

    def pick_gates():
        for u in range(8):
            e = ((half + u) % 2) * 4 + (y + OFFSETS[u // 2]) % 4
            pick = jnp.where(assign_ref[...] == e, gates_ref[...], 0.0)
            picks[u : u + 1, :] = jnp.sum(pick, axis=0, keepdims=True)
        turned = picks[...].T
        for u in range(8):
            gate[u] = jnp.broadcast_to(turned[:, u : u + 1], (TOK, BLK))

    idx_copy = pltpu.make_async_copy(lines, index, idx_sem)

    def fetch_index():
        every = lines.at[pl.ds(0, 7)]
        pltpu.make_async_copy(every, every, r_line).wait()
        idx_copy.start()

    def tiles_of(k, ch, panels=PANELS):
        w = weights[k]
        tiles = []
        for i in range(panels):
            bucket = (ch * panels + i) * 4
            tiles.append(jnp.concatenate(
                [w[s, index[2 * k + s, 0, bucket + g]] for s in range(2) for g in range(4)], axis=0))
        return jnp.concatenate(tiles, axis=1)

    def columns(ch, panels=PANELS):
        return pl.ds(pl.multiple_of(ch * (panels * BLK), panels * BLK), panels * BLK)

    def step(kind, u, h):
        if kind == "own":
            own_slots(u)
            if u == 0:
                place_line()
        elif kind == "dual":
            dual_slots(u)
        elif kind == "hop":
            hop(u, h)
        else:
            to_twin(u, h)

    def chunks(k, between, fresh):
        wait_slots(r_c.at[k], 224)
        partial[...] = jnp.zeros_like(partial)

        def body(ch, carry):
            partial[...] += lax.dot_general(
                tok[:, columns(ch)], tiles_of(k, ch), NT, preferred_element_type=jnp.float32)
            for n, steps in enumerate(between):
                if steps:
                    @pl.when(ch == n)
                    def _():
                        for each in steps:
                            step(*each)
            return carry

        lax.fori_loop(0, CHUNKS, body, 0)
        term = gate[2 * k] * partial[:, 0:BLK] + gate[2 * k + 1] * partial[:, BLK : 2 * BLK]
        total[...] = term if fresh else total[...] + term

    def last_chunks(far):
        rows = pl.ds(pl.multiple_of(((xl + 1) % 2 if far else xl) * HALF, HALF), HALF)
        acc = partial.at[pl.ds(0, HALF)]

        def body(ch, carry):
            tiles = tiles_of(3, ch, LAST_PANELS)
            placed[:, columns(ch, LAST_PANELS)] = tiles
            acc[...] += lax.dot_general(
                tok[rows, columns(ch, LAST_PANELS)], tiles, NT, preferred_element_type=jnp.float32)
            return carry

        if far:
            acc[...] = jnp.zeros_like(acc)
            lax.fori_loop(0, D // (LAST_PANELS * BLK), body, 0)
        else:
            acc[...] = lax.dot_general(tok[rows, :], placed[...], NT, preferred_element_type=jnp.float32)
        term = gate[6, rows, :] * acc[:, 0:BLK] + gate[7, rows, :] * acc[:, BLK : 2 * BLK]
        send_out[rows, :] = (total[rows, :] + term).astype(jnp.bfloat16)
        for n in (2, 1, 3, 0):
            xl_to, y_to = (xl + 1) % 2 if far else xl, (y + n) % 4
            to = pl.ds(pl.multiple_of((xl_to * 4 + y_to) * ROWS, 16), ROWS)
            if far or n > 0:
                send(send_out.at[to], got_out.at[part], s_out, r_out, dev(z, xh, c, xl_to, y_to))
            else:
                got_out[part] = send_out[to, :]

    first = [n for n, each in enumerate(ORDER) if each[0] == "work"]
    for n, each in enumerate(ORDER[: first[0]]):
        step(*each)
        if n == 8:
            pick_gates()
        elif n == 14:
            fetch_index()
    idx_copy.wait()
    tok_copy.wait()
    ends = first[1:] + [len(ORDER)]
    for n in range(0, 3 * CHUNKS, CHUNKS):
        between = [ORDER[lo + 1 : hi] for lo, hi in zip(first[n : n + CHUNKS], ends[n:])]
        chunks(ORDER[first[n]][1], between, n == 0)

    wait_slots(r_c.at[3], 224)
    last_chunks(True)
    last_chunks(False)

    every = lines.at[pl.ds(0, 7)]
    pltpu.make_async_copy(every, every, s_line).wait()
    wait_slots(s_ex, 49)
    for u in range(8):
        wait_slots(s_z.at[u], 7 * (7 + DUAL[u]))
        wait_slots(s_d.at[u], DUAL[u])
        if DUAL[u] < 7:
            wait_slots(s_s.at[u], 8 * (7 - DUAL[u]))
    for k in range(4):
        wait_slots(s_c.at[k], 224)
    seven = got_out.at[pl.ds(0, 7)]
    pltpu.make_async_copy(seven, seven, r_out).wait()
    pltpu.make_async_copy(seven, seven, s_out).wait()

    lanes = lax.broadcasted_iota(jnp.int32, (ROWS, BLK), 1) // PIECE
    for hh in range(2):
        got = [got_out[4 * hh + q].astype(jnp.float32) for q in range(4)]
        for g in range(4):
            tile = got[g]
            for q in range(4):
                if q != g:
                    tile = jnp.where(lanes == q, pltpu.roll(got[q], (q - g) * PIECE % BLK, 1), tile)
                else:
                    tile = jnp.where(lanes == q, got[q], tile)
            lo = g * 2 * BLK + hh * BLK
            out_ref[:, lo : lo + BLK] = tile.astype(jnp.bfloat16)


def on_device(tokens, gates, assign, master, owner):
    dma = pltpu.SemaphoreType.DMA
    vmem = pl.BlockSpec(memory_space=pltpu.VMEM)
    slots = master.shape[1] * lax.axis_size("rep")
    return pl.pallas_call(
        kernel,
        out_shape=jax.ShapeDtypeStruct((ROWS, FW), jnp.bfloat16),
        in_specs=[pl.BlockSpec(memory_space=pltpu.HBM)] * 5,
        out_specs=vmem,
        scratch_shapes=[
            pltpu.VMEM((8, TOK), jnp.float32),
            pltpu.VMEM((8, TOK), jnp.int32),
            pltpu.VMEM(master.shape, jnp.float32),
            pltpu.VMEM(owner.shape, jnp.int32),
            pltpu.VMEM((8, TOK), jnp.float32),
            pltpu.VMEM((TOK, D), jnp.bfloat16),
        ]
        + [pltpu.VMEM((2, slots, PIECE, BLK), jnp.bfloat16)] * 4
        + [
            pltpu.VMEM((2 * BLK, D), jnp.bfloat16),
            pltpu.VMEM((PARTS, SLOTS, PIECE, BLK), jnp.bfloat16),
            pltpu.VMEM((16, BLK), jnp.float32),
            pltpu.VMEM((16, BLK), jnp.float32),
            pltpu.VMEM((1, 256), jnp.int32),
            pltpu.VMEM((8, 1, 256), jnp.int32),
            pltpu.SMEM((8, 1, 256), jnp.int32),
            pltpu.VMEM((8, TOK, BLK), jnp.float32),
            pltpu.VMEM((TOK, 2 * BLK), jnp.float32),
            pltpu.VMEM((TOK, BLK), jnp.float32),
            pltpu.VMEM((TOK, BLK), jnp.bfloat16),
            pltpu.VMEM((PARTS, ROWS, BLK), jnp.bfloat16),
            dma, dma, dma((4,)),
            dma, dma,
            dma, dma((4,)),
            dma((8,)), dma((8, 4)),
            dma((8,)), dma((8,)),
            dma((8,)), dma((8, 5)),
            dma((4,)), dma((4,)),
            dma, dma,
        ],
        compiler_params=pltpu.CompilerParams(
            collective_id=0, has_side_effects=True, vmem_limit_bytes=54 * 1024 * 1024
        ),
        cost_estimate=pl.CostEstimate(
            flops=2 * TOK * D * FW, bytes_accessed=2 * TOK * D + 4 * SLOTS * BLK * 2 * BLK, transcendentals=0
        ),
        name="mixture",
    )(tokens, gates.T, assign.T, master, owner)


def solution(mesh):
    return jax.shard_map(
        on_device,
        mesh=mesh,
        in_specs=(
            P("rep", None),
            P("rep", None),
            P("rep", None),
            P("exp", "rep", None, None),
            P("exp", None),
        ),
        out_specs=P(("rep", "exp"), None),
        check_vma=False,
    )
```
